512 devices in a mesh: row: 32 (over z, y_lo), col: 16 (over x, y_hi, core).
Axes of the slice: x: 4, y: 8 (y_hi: 2, y_lo: 4; y = y_hi * 4 + y_lo), z: 8, core: 2. Of those that a mesh axis runs over, the one named last changes fastest.
Arguments:
- grad_out: bfloat16 [65536, 512], P(('row', 'col')), may hold values from -6 to 6
- relu_mask: int32 [65536, 512], P(('row', 'col')), may hold values 0 or 1
- features: bfloat16 [65536, 512], P(('row', 'col')), may hold values from -6 to 6
- weight: bfloat16 [512, 512], replicated, may hold values from -0.25 to 0.25
- tile_vals: bfloat16 [32, 16, 96, 128, 128], P('row', 'col'), may hold values from -0.1796875 to 0.1796875
- tile_rows: int32 [32, 16, 96], P('row', 'col'), may hold values from 0 to 31, as said below
- tile_cols: int32 [32, 16, 96], P('row', 'col'), may hold values from 0 to 15, as said below
- tile_count: int32 [32, 16], P('row', 'col'), may hold values from 1 to 96, as said below
Outputs:
- grad_in: bfloat16 [65536, 512], P(('row', 'col'))
- grad_weight: float32 [512, 512], replicated
The draws below stay inside these ranges and needn't reach their ends.
Inputs may be any that keep to these rules, and one draw needn't show every extreme that they name: `tile_rows`: within one block, the live slots name distinct pairs of tile row and tile column. `tile_cols`: within one block, the live slots name distinct pairs of tile row and tile column. `tile_count`: some block has all 96 slots live in every draw; loads are skewed over blocks.
All inputs are finite; a program needn't handle non-finite values. No bound on the sum of `relu_mask` on one device may be relied on, other than what follows from the above.
Results may differ from the reference program's by a relative error of at most 0.024.
Values may be sent and summed in bfloat16 or wider, within the bound.
No kernel may reach another device: no remote copies, remote signals or barrier semaphores. Data moves between devices by JAX's collectives and lax.ppermute only.
A program may use at most 64 MiB of HBM per device.

```python
import jax
import jax.numpy as jnp
from jax import lax

WIDTH = 512
TILE = 128
NODE_DEV = 128
GRID_ROWS = 32
GRID_COLS = 16
NODES = 65536
DST_TILES = 32
SRC_TILES = 16
TILE_SLOTS = 96


def tile_places(key):
    keys = jax.random.split(key, GRID_ROWS * GRID_COLS)
    spots = DST_TILES * SRC_TILES

    def one_block(block_key):
        return jax.random.permutation(block_key, spots)[:TILE_SLOTS]
    places = jax.vmap(one_block)(keys)
    return places.reshape(GRID_ROWS, GRID_COLS, TILE_SLOTS).astype(jnp.int32)


def draw_tile_rows(key, part):
    places = tile_places(key)
    return (places // SRC_TILES).astype(jnp.int32)


def draw_tile_cols(key, part):
    places = tile_places(key)
    return (places % SRC_TILES).astype(jnp.int32)


def draw_tile_count(key, part):
    key = jax.random.fold_in(key, 7)
    first_key, second_key, third_key = jax.random.split(key, 3)
    first = jax.random.randint(first_key, (GRID_ROWS * GRID_COLS,), 1, TILE_SLOTS + 1)
    second = jax.random.randint(second_key, (GRID_ROWS * GRID_COLS,), 1, TILE_SLOTS + 1)
    counts = jnp.maximum(first * second // TILE_SLOTS, 1)
    chosen = jax.random.randint(third_key, (), 0, GRID_ROWS * GRID_COLS)
    places = jnp.arange(GRID_ROWS * GRID_COLS, dtype=jnp.int32)
    counts = jnp.where(places == chosen, TILE_SLOTS, counts)
    return counts.reshape(GRID_ROWS, GRID_COLS).astype(jnp.int32)


def set_ends(result, rng, smallest, largest):
    place = [jax.random.randint(jax.random.fold_in(rng, axis), (), 0, length) for axis, length in enumerate(result.shape)]
    longest = result.shape.index(max(result.shape))
    next_to = place[:longest] + [(place[longest] + 1) % result.shape[longest]] + place[longest + 1:]
    return result.at[tuple(place)].set(smallest).at[tuple(next_to)].set(largest)


def block_scale(key, shape, pieces, least, top_value):
    factor_of, own = 1.0, jax.random.fold_in(key, 6)
    for position, blocks in pieces:
        steps = jnp.exp(jax.random.uniform(jax.random.fold_in(own, position), (blocks,), jnp.float32, least / len(pieces), top_value / len(pieces)))
        factor_of = factor_of * jnp.repeat(steps, shape[position] // blocks).reshape([-1 if axis == position else 1 for axis in range(len(shape))])
    return factor_of


def gaussian(own_key, dims, deviation, reach, cuts=(), held_as=jnp.bfloat16):
    gain = block_scale(own_key, dims, cuts, -0.22, 0.18) if cuts else 1.0
    array = jax.random.normal(own_key, dims, jnp.float32) * deviation * gain
    return jnp.minimum(jnp.maximum(array, -reach), reach).astype(held_as)


def setup_inputs(seed: int = 0) -> dict:
    key_list = jax.random.split(jax.random.key(seed), 9)
    grad_out = gaussian(key_list[0], (NODES, WIDTH), 1.0, 6.0, ((0, 512),))
    relu_mask = set_ends((jax.random.randint(key_list[1], (NODES, WIDTH), 0, 2) < 1).astype(jnp.int32), jax.random.fold_in(key_list[1], 1), 0, 1)
    features = gaussian(key_list[2], (NODES, WIDTH), 1.0, 6.0, ((0, 512),))
    weight = gaussian(key_list[3], (WIDTH, WIDTH), WIDTH ** -0.5, 0.25)
    tile_vals = gaussian(key_list[4], (GRID_ROWS, GRID_COLS, TILE_SLOTS, TILE, TILE), 0.03, 0.1796875, ((0, 32), (1, 16)))
    tile_rows = draw_tile_rows(jax.random.fold_in(key_list[8], 71), 0)
    tile_cols = draw_tile_cols(jax.random.fold_in(key_list[8], 71), 0)
    tile_count = draw_tile_count(jax.random.fold_in(key_list[8], 71), 0)
    return dict(grad_out=grad_out, relu_mask=relu_mask, features=features, weight=weight, tile_vals=tile_vals, tile_rows=tile_rows, tile_cols=tile_cols, tile_count=tile_count)


def block_terms(values, rows, cols, count, source):
    def add_one(k, acc):
        piece = source[cols[k]]
        prod = jnp.dot(values[k], piece, preferred_element_type=jnp.float32)
        return acc.at[rows[k]].add(prod)

    start = jnp.zeros((DST_TILES, TILE, WIDTH), jnp.float32)
    return lax.fori_loop(0, count, add_one, start)


def reference(grad_out, relu_mask, features, weight, tile_vals, tile_rows, tile_cols, tile_count):
    slope = (grad_out.astype(jnp.float32) * relu_mask.astype(jnp.float32)).astype(jnp.bfloat16)
    groups = slope.reshape(GRID_ROWS, SRC_TILES, TILE, WIDTH)

    def stripe(column):
        def over_rows(total, row_index):
            part = block_terms(tile_vals[row_index, column], tile_rows[row_index, column],
                               tile_cols[row_index, column], tile_count[row_index, column], groups[row_index])
            rounded = lax.optimization_barrier(part.astype(jnp.bfloat16))
            return total + rounded.astype(jnp.float32), None

        start = jnp.zeros((DST_TILES, TILE, WIDTH), jnp.float32)
        total, _ = lax.scan(over_rows, start, jnp.arange(GRID_ROWS, dtype=jnp.int32))
        return total

    stripes = lax.map(stripe, jnp.arange(GRID_COLS, dtype=jnp.int32))
    stripes = stripes.reshape(GRID_COLS, GRID_ROWS, NODE_DEV, WIDTH).transpose(1, 0, 2, 3)
    aggregated = stripes.reshape(NODES, WIDTH).astype(jnp.bfloat16)
    grad_in = jnp.dot(aggregated, weight.T, preferred_element_type=jnp.float32).astype(jnp.bfloat16)
    grad_weight = jnp.dot(features.T, aggregated, preferred_element_type=jnp.float32)
    return grad_in, grad_weight
```

```python
import jax
import jax.numpy as jnp
import numpy as np
from jax import lax
from jax.experimental import pallas as pl
from jax.experimental.pallas import tpu as pltpu
from jax.sharding import Mesh, PartitionSpec as P

SIZES = (8, 4, 4, 2, 2)
AXES = ("z", "y", "x", "h", "k")
UNROLL = 8
VMEM_LIMIT = 48 << 20

SMEM_SPEC = pl.BlockSpec(memory_space=pltpu.SMEM)
VMEM_SPEC = pl.BlockSpec(memory_space=pltpu.VMEM)


def permute(value, move):
    pairs = []
    for index, place in enumerate(np.ndindex(*SIZES)):
        pairs.append((index, int(np.ravel_multi_index(move(*place), SIZES))))
    return lax.ppermute(value, AXES, pairs)


def h_swap(z, y, x, h, k):
    return (z, y, x, 1 - h, k)


def k_swap(z, y, x, h, k):
    return (z, y, x, h, 1 - k)


def x_from(step):
    def move(z, y, x, h, k):
        return (z, y, (x - step) % 4, h, k)

    return move


def kernel_call(kernel, out_shape, in_specs, scratch=(), name=None):
    return pl.pallas_call(
        kernel,
        out_shape=out_shape,
        in_specs=in_specs,
        out_specs=jax.tree.map(lambda _: VMEM_SPEC, out_shape),
        scratch_shapes=list(scratch),
        compiler_params=pltpu.CompilerParams(vmem_limit_bytes=VMEM_LIMIT),
        name=name,
    )


def block_kernel(count, rows, places, vals, own, other, out, acc, source):
    source[0:8] = own[...]
    source[8:16] = other[...]
    acc[...] = jnp.zeros_like(acc)
    live = count[0]

    def group(index, carry):
        terms = []
        for step in range(UNROLL):
            slot = index * UNROLL + step
            place = places[slot]
            term = jnp.dot(vals[slot], source[place], preferred_element_type=jnp.float32)
            terms.append((rows[slot], jnp.where(slot < live, term, 0.0)))
        for row, term in terms:
            acc[row] += term
        return carry

    lax.fori_loop(0, pl.cdiv(live, UNROLL), group, 0)
    out[...] = acc[...].astype(jnp.bfloat16)


def node_kernel(parts, weight, grad_in, agg_t):
    total = parts[0].astype(jnp.float32)
    for index in range(1, 4):
        total = total + parts[index].astype(jnp.float32)
    agg = total.astype(jnp.bfloat16)
    grad_in[...] = lax.dot_general(
        agg, weight[...], (((1,), (1,)), ((), ())), preferred_element_type=jnp.float32
    ).astype(jnp.bfloat16)
    agg_t[...] = agg.astype(jnp.float32).T.astype(jnp.bfloat16).reshape(8, 64, 128)


def slice_kernel(agg_t, features, out):
    total = jnp.zeros((64, 512), jnp.float32)
    for index in range(8):
        total += jnp.dot(agg_t[index], features[index], preferred_element_type=jnp.float32)
    for index in range(4):
        out[:, index, :] = total[:, 128 * index:128 * (index + 1)]


def sum_kernel(parts, out):
    total = jnp.sum(parts[...], axis=0)
    out[...] = jnp.broadcast_to(total[None], out.shape)


def last_kernel(at, own, other, out, whole):
    x, k = at[0], at[1]
    for step in range(4):
        chip = lax.rem(x + step, 4)
        whole[chip * 2 + k] = own[step]
        whole[chip * 2 + 1 - k] = other[step]
    out[...] = whole[...].reshape(512, 512).astype(jnp.float32).T


def body(grad_out, relu_mask, features, weight, tile_vals, tile_rows, tile_cols, tile_count):
    x, h, k = (lax.axis_index(name) for name in ("x", "h", "k"))
    slope = (grad_out.astype(jnp.float32) * relu_mask.astype(jnp.float32)).astype(jnp.bfloat16)

    pair = jnp.stack([slope, permute(slope, h_swap)])
    own = jnp.concatenate([pair] + [permute(pair, x_from(step)) for step in (1, 2, 3)])
    other = permute(own, k_swap)
    cols = tile_cols[0, 0]
    places = ((cols // 4 - x) % 4) * 2 + ((cols // 2 % 2) ^ h) + 8 * ((cols % 2) ^ k)

    terms = kernel_call(
        block_kernel,
        jax.ShapeDtypeStruct((32, 128, 512), jnp.bfloat16),
        [SMEM_SPEC] * 3 + [VMEM_SPEC] * 3,
        [pltpu.VMEM((32, 128, 512), jnp.float32), pltpu.VMEM((16, 128, 512), jnp.bfloat16)],
        name="block_terms",
    )(tile_count[0], tile_rows[0, 0], places, tile_vals[0, 0], own, other)

    parts = lax.psum_scatter(terms, "z", scatter_dimension=0, tiled=True)
    parts = lax.all_to_all(parts, "y", 0, 0, tiled=True)
    grad_in, agg_t = kernel_call(
        node_kernel,
        (jax.ShapeDtypeStruct((128, 512), jnp.bfloat16), jax.ShapeDtypeStruct((8, 64, 128), jnp.bfloat16)),
        [VMEM_SPEC] * 2,
        name="nodes",
    )(parts, weight)

    gathered = lax.all_gather(features, ("x", "k"), axis=0, tiled=False)
    agg_t = lax.all_to_all(agg_t, ("x", "k"), 0, 0, tiled=True)
    share = kernel_call(
        slice_kernel, jax.ShapeDtypeStruct((64, 4, 128), jnp.float32), [VMEM_SPEC] * 2, name="weight_slice"
    )(agg_t, gathered)
    share = lax.all_to_all(share, ("z", "y", "h"), 0, 0, tiled=True)
    share = kernel_call(
        sum_kernel, jax.ShapeDtypeStruct((64, 4, 128), jnp.float32), [VMEM_SPEC], name="weight_sum"
    )(share)
    share = lax.all_to_all(share, ("z", "y", "h"), 0, 0, tiled=True)
    share = share.reshape(1, 64, 512).astype(jnp.bfloat16)
    own = jnp.concatenate([share] + [permute(share, x_from(step)) for step in (1, 2, 3)])
    other = permute(own, k_swap)
    grad_weight = kernel_call(
        last_kernel,
        jax.ShapeDtypeStruct((512, 512), jnp.float32),
        [SMEM_SPEC] + [VMEM_SPEC] * 2,
        [pltpu.VMEM((8, 64, 512), jnp.bfloat16)],
        name="weight_order",
    )(jnp.stack([x, k]), own, other)
    return (grad_in, grad_weight)


def solution(mesh):
    fine = Mesh(mesh.devices.reshape(SIZES), AXES)
    nodes = P(AXES, None)
    rows, cols = AXES[:2], AXES[2:]
    return jax.shard_map(
        body,
        mesh=fine,
        in_specs=(
            nodes,
            nodes,
            nodes,
            P(),
            P(rows, cols, None, None, None),
            P(rows, cols, None),
            P(rows, cols, None),
            P(rows, cols),
        ),
        out_specs=(nodes, P()),
        check_vma=False,
    )
```

```python
import functools

import jax
import jax.numpy as jnp
import numpy as np
from jax import lax
from jax.experimental import pallas as pl
from jax.experimental.pallas import tpu as pltpu
from jax.sharding import Mesh, PartitionSpec as P

SIZES = (8, 4, 4, 2, 2)
AXES = ("z", "y", "x", "h", "k")
UNROLL = 24
SLOTS = 96
HALF = 64
WIDTH = 512
VMEM_LIMIT = 16 << 20
VMEM_WHOLE = 48 << 20

SMEM_SPEC = pl.BlockSpec(memory_space=pltpu.SMEM)
VMEM_SPEC = pl.BlockSpec(memory_space=pltpu.VMEM)


def permute(value, move):
    pairs = []
    for index, place in enumerate(np.ndindex(*SIZES)):
        pairs.append((index, int(np.ravel_multi_index(move(*place), SIZES))))
    return lax.ppermute(value, AXES, pairs)


def h_swap(z, y, x, h, k):
    return (z, y, x, 1 - h, k)


def k_swap(z, y, x, h, k):
    return (z, y, x, h, 1 - k)


def x_from(step):
    def move(z, y, x, h, k):
        return (z, y, (x - step) % 4, h, k)

    return move


def y_from(step):
    def move(z, y, x, h, k):
        return (z, (y - step) % 4, x, h, k)

    return move


def y_flip(bit):
    def move(z, y, x, h, k):
        return (z, y ^ bit, x, h, k)

    return move


def z_up(z, y, x, h, k):
    return ((z + 1) % 8, y, x, h, k)


def z_down(z, y, x, h, k):
    return ((z - 1) % 8, y, x, h, k)


def kernel_call(kernel, out_shape, in_specs, scratch=(), name=None, limit=VMEM_LIMIT, out_specs=None):
    return pl.pallas_call(
        kernel,
        out_shape=out_shape,
        in_specs=in_specs,
        out_specs=out_specs or jax.tree.map(lambda _: VMEM_SPEC, out_shape),
        scratch_shapes=list(scratch),
        compiler_params=pltpu.CompilerParams(vmem_limit_bytes=limit),
        name=name,
    )


def block_kernel(at, codes, vals, own, own_h, other, other_h, *refs):
    pieces, (acc, source, held, sem) = refs[:9], refs[9:]
    copy = pltpu.make_async_copy(vals, held, sem)
    copy.start()
    for index, blocks in enumerate((own, own_h, other, other_h)):
        source[4 * index:4 * index + 4] = blocks[...]
    acc[...] = jnp.zeros_like(acc)
    copy.wait()

    def group(index, carry):
        terms = []
        for step in range(UNROLL):
            slot = index * UNROLL + step
            code = codes[slot]
            term = jnp.dot(held[slot], source[code % 16], preferred_element_type=jnp.float32)
            terms.append((code // 16, term))
        for row, term in terms:
            acc[row] += term
        return carry

    lax.fori_loop(0, pl.cdiv(codes[SLOTS], UNROLL), group, 0)

    def chunk(step, rows=slice(None)):
        return acc[pl.ds(4 * lax.rem(at[0] + step, 8), 4), rows].astype(jnp.bfloat16)

    pieces[0][...] = chunk(4, slice(0, HALF))
    pieces[1][...] = chunk(4, slice(HALF, 128))
    for piece, step in zip(pieces[2:], (3, 5, 2, 6, 1, 7, 0)):
        piece[...] = chunk(step)


def add_kernel(first, piece, came, *refs):
    out = refs[-1]
    rows = slice(first, first + came.shape[1])
    if came.shape != piece.shape:
        out[...] = piece[...]
    out[:, rows] = (piece[:, rows].astype(jnp.float32) + came[...].astype(jnp.float32)).astype(jnp.bfloat16)


def add(piece, came, first=0, after=()):
    return kernel_call(
        functools.partial(add_kernel, first),
        jax.ShapeDtypeStruct(piece.shape, jnp.bfloat16),
        [VMEM_SPEC] * 2 + [pl.BlockSpec(memory_space=pl.ANY)] * len(after),
        name="ring_add",
    )(piece, came, *after)


def product_kernel(at, features, along_1, along_2, along_3, parts, keep, send, across, total):
    y, k = at[1], at[2]
    total[...] = jnp.zeros_like(total)
    for step, nodes in enumerate((features, along_1, along_2, along_3)):
        total[...] += lax.dot_general(
            nodes[...], parts[lax.rem(y + step, 4)], (((0,), (0,)), ((), ())), preferred_element_type=jnp.float32
        )
    keep[...] = total[pl.ds(pl.multiple_of(256 * k, 256), 256), :]
    send[...] = total[pl.ds(pl.multiple_of(256 * (1 - k), 256), 256), :].astype(jnp.bfloat16)
    for index in range(2):
        across[index] = parts[2 * index + 1 - lax.rem(y, 2)]


def half_kernel(keep, came, out):
    out[...] = (keep[...] + came[...].astype(jnp.float32)).astype(jnp.bfloat16).reshape(out.shape)


def sum_kernel(parts, out):
    total = parts[0].astype(jnp.float32)
    for index in range(1, parts.shape[0]):
        total = total + parts[index].astype(jnp.float32)
    total = total.astype(out.dtype)
    for index in range(out.shape[0]):
        out[index] = total


def share_kernel(at, half, parts, came, out, keep, send):
    sum_kernel(half, out)
    odd, high = lax.rem(at[1], 2), at[1] // 2

    def pair(index):
        return parts[2 * index + odd].astype(jnp.float32) + came[index].astype(jnp.float32)

    keep[...] = pair(high)
    send[...] = pair(1 - high).astype(jnp.bfloat16)


def total_kernel(share, keep, came, weight, out, grad_in):
    sum_kernel(share, out)
    agg = (keep[...] + came[...].astype(jnp.float32)).astype(jnp.bfloat16)
    grad_in[...] = lax.dot_general(
        agg, weight[...], (((1,), (1,)), ((), ())), preferred_element_type=jnp.float32
    ).astype(jnp.bfloat16)


def last_kernel(at, own, other, out):
    k = at[2]
    out[pl.ds(pl.multiple_of(256 * k, 256), 256), :] = own[...].reshape(256, WIDTH).astype(jnp.float32)
    out[pl.ds(pl.multiple_of(256 * (1 - k), 256), 256), :] = other[...].reshape(256, WIDTH).astype(jnp.float32)


def body(grad_out, relu_mask, features, weight, tile_vals, tile_rows, tile_cols, tile_count):
    x, h, k = (lax.axis_index(name) for name in ("x", "h", "k"))
    slope = (grad_out.astype(jnp.float32) * relu_mask.astype(jnp.float32)).astype(jnp.bfloat16)

    slope_h = permute(slope, h_swap)
    own = jnp.stack([slope] + [permute(slope, x_from(step)) for step in (1, 2, 3)])
    other = permute(own, k_swap)
    own_h = jnp.stack([slope_h] + [permute(slope_h, x_from(step)) for step in (1, 2, 3)])
    other_h = permute(own_h, k_swap)
    cols = tile_cols[0, 0]
    places = (cols // 4 - x) % 4 + 4 * ((cols // 2 % 2) ^ h) + 8 * ((cols % 2) ^ k)

    live = jnp.arange(SLOTS, dtype=jnp.int32) < tile_count[0, 0]
    codes = jnp.concatenate([jnp.where(live, tile_rows[0, 0], 32) * 16 + places, tile_count[0]])
    at = jnp.stack([lax.axis_index("z"), lax.axis_index("y"), k])
    piece = jax.ShapeDtypeStruct((4, 128, WIDTH), jnp.bfloat16)
    first = [
        jax.ShapeDtypeStruct((4, HALF, WIDTH), jnp.bfloat16),
        jax.ShapeDtypeStruct((4, 128 - HALF, WIDTH), jnp.bfloat16),
    ]
    pieces = kernel_call(
        block_kernel,
        first + [piece] * 7,
        [SMEM_SPEC] * 2 + [pl.BlockSpec(memory_space=pl.ANY)] + [VMEM_SPEC] * 4,
        [
            pltpu.VMEM((33, 128, WIDTH), jnp.float32),
            pltpu.VMEM((16, 128, WIDTH), jnp.bfloat16),
            pltpu.VMEM((SLOTS, 128, 128), jnp.bfloat16),
            pltpu.SemaphoreType.DMA,
        ],
        name="block_terms",
        limit=VMEM_WHOLE,
    )(at, codes, tile_vals[0, 0], own, own_h, other, other_h)

    along = [permute(features, y_from(step)) for step in (1, 2, 3)]
    up, down = pieces[0], pieces[1]
    for step in range(4):
        up, down = permute(up, z_up), permute(down, z_down)
        after = along[step - 1:step] if step else []
        if step == 0:
            up, down = add(pieces[2], up), add(pieces[3], down, HALF)
        elif step < 3:
            up, down = add(pieces[2 + 2 * step], up, 0, after), add(pieces[3 + 2 * step], down)
    parts = (
        pieces[8].astype(jnp.float32) + up.astype(jnp.float32) + down.astype(jnp.float32)
    ).astype(jnp.bfloat16)

    keep, send, across = kernel_call(
        product_kernel,
        (
            jax.ShapeDtypeStruct((256, WIDTH), jnp.float32),
            jax.ShapeDtypeStruct((256, WIDTH), jnp.bfloat16),
            jax.ShapeDtypeStruct((2, 128, WIDTH), jnp.bfloat16),
        ),
        [SMEM_SPEC] + [VMEM_SPEC] * 5,
        [pltpu.VMEM((WIDTH, WIDTH), jnp.float32)],
        name="weight_product",
    )(at, features, *along, parts)
    half = kernel_call(
        half_kernel, jax.ShapeDtypeStruct((32, 8, WIDTH), jnp.bfloat16), [VMEM_SPEC] * 2, name="weight_half"
    )(keep, permute(send, k_swap))
    half = lax.all_to_all(half, ("z", "x"), 0, 0, tiled=True)
    share, keep, send = kernel_call(
        share_kernel,
        (
            jax.ShapeDtypeStruct((8, 8, WIDTH), jnp.bfloat16),
            jax.ShapeDtypeStruct((128, WIDTH), jnp.float32),
            jax.ShapeDtypeStruct((128, WIDTH), jnp.bfloat16),
        ),
        [SMEM_SPEC] + [VMEM_SPEC] * 3,
        name="weight_share",
    )(at, half, parts, permute(across, y_flip(1)))
    send = permute(send, y_flip(2))
    share = lax.all_to_all(share, ("y", "h"), 0, 0, tiled=True)
    half, grad_in = kernel_call(
        total_kernel,
        (jax.ShapeDtypeStruct((32, 8, WIDTH), jnp.bfloat16), jax.ShapeDtypeStruct((128, WIDTH), jnp.bfloat16)),
        [VMEM_SPEC] * 4,
        name="weight_total",
    )(share, keep, send, weight)
    half = lax.all_to_all(half, ("z", "x"), 0, 0, tiled=True)
    grad_weight = kernel_call(
        last_kernel,
        jax.ShapeDtypeStruct((WIDTH, WIDTH), jnp.float32),
        [SMEM_SPEC] + [VMEM_SPEC] * 2,
        name="weight_order",
    )(at, half, permute(half, k_swap))
    return (grad_in, grad_weight)


def solution(mesh):
    fine = Mesh(mesh.devices.reshape(SIZES), AXES)
    nodes = P(AXES, None)
    rows, cols = AXES[:2], AXES[2:]
    return jax.shard_map(
        body,
        mesh=fine,
        in_specs=(
            nodes,
            nodes,
            nodes,
            P(),
            P(rows, cols, None, None, None),
            P(rows, cols, None),
            P(rows, cols, None),
            P(rows, cols),
        ),
        out_specs=(nodes, P()),
        check_vma=False,
    )
```

```python
import functools

import jax
import jax.numpy as jnp
import numpy as np
from jax import lax
from jax.experimental import pallas as pl
from jax.experimental.pallas import tpu as pltpu
from jax.sharding import Mesh, PartitionSpec as P

SIZES = (8, 4, 4, 2, 2)
AXES = ("z", "y", "x", "h", "k")
UNROLL = 24
SLOTS = 96
HALF = 64
WIDTH = 512
VMEM_LIMIT = 16 << 20
VMEM_WHOLE = 48 << 20

SMEM_SPEC = pl.BlockSpec(memory_space=pltpu.SMEM)
VMEM_SPEC = pl.BlockSpec(memory_space=pltpu.VMEM)


def permute(value, move):
    pairs = []
    for index, place in enumerate(np.ndindex(*SIZES)):
        pairs.append((index, int(np.ravel_multi_index(move(*place), SIZES))))
    return lax.ppermute(value, AXES, pairs)


def h_swap(z, y, x, h, k):
    return (z, y, x, 1 - h, k)


def k_swap(z, y, x, h, k):
    return (z, y, x, h, 1 - k)


def x_from(step):
    def move(z, y, x, h, k):
        return (z, y, (x - step) % 4, h, k)

    return move


def around(block):
    far = permute(block, x_from(2))
    return [block, permute(block, x_from(1)), far, permute(block, x_from(3))]


def y_from(step):
    def move(z, y, x, h, k):
        return (z, (y - step) % 4, x, h, k)

    return move


def y_flip(bit):
    def move(z, y, x, h, k):
        return (z, y ^ bit, x, h, k)

    return move


def z_up(z, y, x, h, k):
    return ((z + 1) % 8, y, x, h, k)


def z_down(z, y, x, h, k):
    return ((z - 1) % 8, y, x, h, k)


def kernel_call(kernel, out_shape, in_specs, scratch=(), name=None, limit=VMEM_LIMIT, out_specs=None):
    return pl.pallas_call(
        kernel,
        out_shape=out_shape,
        in_specs=in_specs,
        out_specs=out_specs or jax.tree.map(lambda _: VMEM_SPEC, out_shape),
        scratch_shapes=list(scratch),
        compiler_params=pltpu.CompilerParams(vmem_limit_bytes=limit),
        name=name,
    )


def block_kernel(at, codes, vals, own, own_h, other, other_h, *refs):
    pieces, (acc, source, held, sems) = refs[-13:-4], refs[-4:]
    copies = [pltpu.make_async_copy(vals, held, sems.at[4])]
    for index, blocks in enumerate((own, own_h, other, other_h)):
        copies.append(pltpu.make_async_copy(blocks, source.at[pl.ds(4 * index, 4)], sems.at[index]))
    for copy in copies:
        copy.start()
    acc[...] = jnp.zeros_like(acc)
    for copy in copies:
        copy.wait()

    def group(index, carry):
        terms = []
        for step in range(UNROLL):
            slot = index * UNROLL + step
            code = codes[slot]
            term = jnp.dot(held[slot], source[code % 16], preferred_element_type=jnp.float32)
            terms.append((code // 16, term))
        for row, term in terms:
            acc[row] += term
        return carry

    lax.fori_loop(0, pl.cdiv(codes[SLOTS], UNROLL), group, 0)

    def chunk(step, rows=slice(None)):
        return acc[pl.ds(4 * lax.rem(at[0] + step, 8), 4), rows].astype(jnp.bfloat16)

    pieces[0][...] = chunk(4, slice(0, HALF))
    pieces[1][...] = chunk(4, slice(HALF, 128))
    for piece, step in zip(pieces[2:], (3, 5, 2, 6, 1, 7, 0)):
        piece[...] = chunk(step)


def add_kernel(first, piece, came, *refs):
    out = refs[-1]
    rows = slice(first, first + came.shape[1])
    if came.shape != piece.shape:
        out[...] = piece[...]
    out[:, rows] = (piece[:, rows].astype(jnp.float32) + came[...].astype(jnp.float32)).astype(jnp.bfloat16)


def add(piece, came, first=0, after=()):
    return kernel_call(
        functools.partial(add_kernel, first),
        jax.ShapeDtypeStruct(piece.shape, jnp.bfloat16),
        [VMEM_SPEC] * 2 + [pl.BlockSpec(memory_space=pl.ANY)] * len(after),
        name="ring_add",
    )(piece, came, *after)


def product_kernel(at, features, along_1, along_2, along_3, parts, keep, send, across, total):
    y, k = at[1], at[2]
    total[...] = jnp.zeros_like(total)
    for step, nodes in enumerate((features, along_1, along_2, along_3)):
        total[...] += lax.dot_general(
            nodes[...], parts[lax.rem(y + step, 4)], (((0,), (0,)), ((), ())), preferred_element_type=jnp.float32
        )
    keep[...] = total[pl.ds(pl.multiple_of(256 * k, 256), 256), :]
    send[...] = total[pl.ds(pl.multiple_of(256 * (1 - k), 256), 256), :].astype(jnp.bfloat16)
    for index in range(2):
        across[index] = parts[2 * index + 1 - lax.rem(y, 2)]


def half_kernel(keep, came, out):
    out[...] = (keep[...] + came[...].astype(jnp.float32)).astype(jnp.bfloat16).reshape(out.shape)


def sum_kernel(parts, out):
    total = parts[0].astype(jnp.float32)
    for index in range(1, parts.shape[0]):
        total = total + parts[index].astype(jnp.float32)
    total = total.astype(out.dtype)
    for index in range(out.shape[0]):
        out[index] = total


def share_kernel(at, half, parts, came, out, keep, send):
    sum_kernel(half, out)
    odd, high = lax.rem(at[1], 2), at[1] // 2

    def pair(index):
        return parts[2 * index + odd].astype(jnp.float32) + came[index].astype(jnp.float32)

    keep[...] = pair(high)
    send[...] = pair(1 - high).astype(jnp.bfloat16)


def total_kernel(share, keep, came, weight, out, grad_in):
    sum_kernel(share, out)
    agg = (keep[...] + came[...].astype(jnp.float32)).astype(jnp.bfloat16)
    grad_in[...] = lax.dot_general(
        agg, weight[...], (((1,), (1,)), ((), ())), preferred_element_type=jnp.float32
    ).astype(jnp.bfloat16)


def last_kernel(at, own, other, out):
    k = at[2]
    out[pl.ds(pl.multiple_of(256 * k, 256), 256), :] = own[...].reshape(256, WIDTH).astype(jnp.float32)
    out[pl.ds(pl.multiple_of(256 * (1 - k), 256), 256), :] = other[...].reshape(256, WIDTH).astype(jnp.float32)


def body(grad_out, relu_mask, features, weight, tile_vals, tile_rows, tile_cols, tile_count):
    x, h, k = (lax.axis_index(name) for name in ("x", "h", "k"))
    slope = (grad_out.astype(jnp.float32) * relu_mask.astype(jnp.float32)).astype(jnp.bfloat16)

    slope_h = permute(slope, h_swap)
    own = jnp.stack(around(slope))
    other = permute(own, k_swap)
    own_h = jnp.stack(around(slope_h))
    other_h = permute(own_h, k_swap)
    cols = tile_cols[0, 0]
    places = (cols // 4 - x) % 4 + 4 * ((cols // 2 % 2) ^ h) + 8 * ((cols % 2) ^ k)

    live = jnp.arange(SLOTS, dtype=jnp.int32) < tile_count[0, 0]
    codes = jnp.concatenate([jnp.where(live, tile_rows[0, 0] * 16 + places, 32 * 16), tile_count[0]])
    at = jnp.stack([lax.axis_index("z"), lax.axis_index("y"), k])
    piece = jax.ShapeDtypeStruct((4, 128, WIDTH), jnp.bfloat16)
    first = [
        jax.ShapeDtypeStruct((4, HALF, WIDTH), jnp.bfloat16),
        jax.ShapeDtypeStruct((4, 128 - HALF, WIDTH), jnp.bfloat16),
    ]
    pieces = kernel_call(
        block_kernel,
        first + [piece] * 7,
        [SMEM_SPEC] * 2 + [pl.BlockSpec(memory_space=pl.ANY)] * 5,
        [
            pltpu.VMEM((33, 128, WIDTH), jnp.float32),
            pltpu.VMEM((16, 128, WIDTH), jnp.bfloat16),
            pltpu.VMEM((SLOTS, 128, 128), jnp.bfloat16),
            pltpu.SemaphoreType.DMA((5,)),
        ],
        name="block_terms",
        limit=VMEM_WHOLE,
    )(at, codes, tile_vals[0, 0], own, own_h, other, other_h)

    along = [permute(features, y_from(step)) for step in (1, 2, 3)]
    up, down = pieces[0], pieces[1]
    for step in range(4):
        up, down = permute(up, z_up), permute(down, z_down)
        after = along[step - 1:step] if step else []
        if step == 0:
            up, down = add(pieces[2], up), add(pieces[3], down, HALF)
        elif step < 3:
            up, down = add(pieces[2 + 2 * step], up), add(pieces[3 + 2 * step], down, 0, after)
    parts = (
        pieces[8].astype(jnp.float32) + up.astype(jnp.float32) + down.astype(jnp.float32)
    ).astype(jnp.bfloat16)

    keep, send, across = kernel_call(
        product_kernel,
        (
            jax.ShapeDtypeStruct((256, WIDTH), jnp.float32),
            jax.ShapeDtypeStruct((256, WIDTH), jnp.bfloat16),
            jax.ShapeDtypeStruct((2, 128, WIDTH), jnp.bfloat16),
        ),
        [SMEM_SPEC] + [VMEM_SPEC] * 5,
        [pltpu.VMEM((WIDTH, WIDTH), jnp.float32)],
        name="weight_product",
    )(at, features, *along, parts)
    half = kernel_call(
        half_kernel, jax.ShapeDtypeStruct((32, 8, WIDTH), jnp.bfloat16), [VMEM_SPEC] * 2, name="weight_half"
    )(keep, permute(send, k_swap))
    half = lax.all_to_all(half, ("z", "x"), 0, 0, tiled=True)
    share, keep, send = kernel_call(
        share_kernel,
        (
            jax.ShapeDtypeStruct((8, 8, WIDTH), jnp.bfloat16),
            jax.ShapeDtypeStruct((128, WIDTH), jnp.float32),
            jax.ShapeDtypeStruct((128, WIDTH), jnp.bfloat16),
        ),
        [SMEM_SPEC] + [VMEM_SPEC] * 3,
        name="weight_share",
    )(at, half, parts, permute(across, y_flip(1)))
    send = permute(send, y_flip(2))
    share = lax.all_to_all(share, ("y", "h"), 0, 0, tiled=True)
    half, grad_in = kernel_call(
        total_kernel,
        (jax.ShapeDtypeStruct((32, 8, WIDTH), jnp.bfloat16), jax.ShapeDtypeStruct((128, WIDTH), jnp.bfloat16)),
        [VMEM_SPEC] * 4,
        name="weight_total",
    )(share, keep, send, weight)
    half = lax.all_to_all(half, ("z", "x"), 0, 0, tiled=True)
    grad_weight = kernel_call(
        last_kernel,
        jax.ShapeDtypeStruct((WIDTH, WIDTH), jnp.float32),
        [SMEM_SPEC] + [VMEM_SPEC] * 2,
        name="weight_order",
    )(at, half, permute(half, k_swap))
    return (grad_in, grad_weight)


def solution(mesh):
    fine = Mesh(mesh.devices.reshape(SIZES), AXES)
    nodes = P(AXES, None)
    rows, cols = AXES[:2], AXES[2:]
    return jax.shard_map(
        body,
        mesh=fine,
        in_specs=(
            nodes,
            nodes,
            nodes,
            P(),
            P(rows, cols, None, None, None),
            P(rows, cols, None),
            P(rows, cols, None),
            P(rows, cols),
        ),
        out_specs=(nodes, P()),
        check_vma=False,
    )
```

```python
import functools

import jax
import jax.numpy as jnp
import numpy as np
from jax import lax
from jax.experimental import pallas as pl
from jax.experimental.pallas import tpu as pltpu
from jax.sharding import Mesh, PartitionSpec as P

SIZES = (8, 4, 4, 2, 2)
AXES = ("z", "y", "x", "h", "k")
UNROLL = 24
SLOTS = 96
HALF = 64
WIDTH = 512
VMEM_LIMIT = 16 << 20
VMEM_WHOLE = 48 << 20

SMEM_SPEC = pl.BlockSpec(memory_space=pltpu.SMEM)
VMEM_SPEC = pl.BlockSpec(memory_space=pltpu.VMEM)


def permute(value, move):
    pairs = []
    for index, place in enumerate(np.ndindex(*SIZES)):
        pairs.append((index, int(np.ravel_multi_index(move(*place), SIZES))))
    return lax.ppermute(value, AXES, pairs)


def h_swap(z, y, x, h, k):
    return (z, y, x, 1 - h, k)


def k_swap(z, y, x, h, k):
    return (z, y, x, h, 1 - k)


def x_from(step):
    def move(z, y, x, h, k):
        return (z, y, (x - step) % 4, h, k)

    return move


def around(block):
    far = permute(block, x_from(2))
    return [block, permute(block, x_from(1)), far, permute(block, x_from(3))]


def y_from(step):
    def move(z, y, x, h, k):
        return (z, (y - step) % 4, x, h, k)

    return move


def y_flip(bit):
    def move(z, y, x, h, k):
        return (z, y ^ bit, x, h, k)

    return move


def z_up(z, y, x, h, k):
    return ((z + 1) % 8, y, x, h, k)


def z_down(z, y, x, h, k):
    return ((z - 1) % 8, y, x, h, k)


def kernel_call(kernel, out_shape, in_specs, scratch=(), name=None, limit=VMEM_LIMIT, out_specs=None):
    return pl.pallas_call(
        kernel,
        out_shape=out_shape,
        in_specs=in_specs,
        out_specs=out_specs or jax.tree.map(lambda _: VMEM_SPEC, out_shape),
        scratch_shapes=list(scratch),
        compiler_params=pltpu.CompilerParams(vmem_limit_bytes=limit),
        name=name,
    )


def block_kernel(at, codes, vals, own, own_h, other, other_h, *refs):
    pieces, (acc, source, held, sems) = refs[-13:-4], refs[-4:]
    copies = [pltpu.make_async_copy(vals, held, sems.at[4])]
    for index, blocks in enumerate((own, own_h, other, other_h)):
        copies.append(pltpu.make_async_copy(blocks, source.at[pl.ds(4 * index, 4)], sems.at[index]))
    for copy in copies:
        copy.start()
    acc[...] = jnp.zeros_like(acc)
    for copy in copies:
        copy.wait()

    def group(index, carry):
        terms = []
        for step in range(UNROLL):
            slot = index * UNROLL + step
            code = codes[slot]
            term = jnp.dot(held[slot], source[code % 16], preferred_element_type=jnp.float32)
            terms.append((code // 16, term))
        for row, term in terms:
            acc[row] += term
        return carry

    lax.fori_loop(0, pl.cdiv(at[3], UNROLL), group, 0)

    def chunk(step, rows=slice(None)):
        return acc[pl.ds(4 * lax.rem(at[0] + step, 8), 4), rows].astype(jnp.bfloat16)

    pieces[0][...] = chunk(4, slice(0, HALF))
    pieces[1][...] = chunk(4, slice(HALF, 128))
    for piece, step in zip(pieces[2:], (3, 5, 2, 6, 1, 7, 0)):
        piece[...] = chunk(step)


def add_kernel(first, piece, came, *refs):
    out = refs[-1]
    rows = slice(first, first + came.shape[1])
    if came.shape != piece.shape:
        out[...] = piece[...]
    out[:, rows] = (piece[:, rows].astype(jnp.float32) + came[...].astype(jnp.float32)).astype(jnp.bfloat16)


def add(piece, came, first=0, after=()):
    return kernel_call(
        functools.partial(add_kernel, first),
        jax.ShapeDtypeStruct(piece.shape, jnp.bfloat16),
        [VMEM_SPEC] * 2 + [pl.BlockSpec(memory_space=pl.ANY)] * len(after),
        name="ring_add",
    )(piece, came, *after)


def product_kernel(at, features, along_1, along_2, along_3, parts, keep, send, across, total):
    y, k = at[1], at[2]
    total[...] = jnp.zeros_like(total)
    for step, nodes in enumerate((features, along_1, along_2, along_3)):
        total[...] += lax.dot_general(
            nodes[...], parts[lax.rem(y + step, 4)], (((0,), (0,)), ((), ())), preferred_element_type=jnp.float32
        )
    keep[...] = total[pl.ds(pl.multiple_of(256 * k, 256), 256), :]
    send[...] = total[pl.ds(pl.multiple_of(256 * (1 - k), 256), 256), :].astype(jnp.bfloat16)
    for index in range(2):
        across[index] = parts[2 * index + 1 - lax.rem(y, 2)]


def half_kernel(keep, came, out):
    out[...] = (keep[...] + came[...].astype(jnp.float32)).astype(jnp.bfloat16).reshape(out.shape)


def sum_kernel(parts, out):
    total = parts[0].astype(jnp.float32)
    for index in range(1, parts.shape[0]):
        total = total + parts[index].astype(jnp.float32)
    total = total.astype(out.dtype)
    for index in range(out.shape[0]):
        out[index] = total


def share_kernel(at, half, parts, came, out, keep, send):
    sum_kernel(half, out)
    odd, high = lax.rem(at[1], 2), at[1] // 2

    def pair(index):
        return parts[2 * index + odd].astype(jnp.float32) + came[index].astype(jnp.float32)

    keep[...] = pair(high)
    send[...] = pair(1 - high).astype(jnp.bfloat16)


def total_kernel(share, keep, came, weight, out, grad_in):
    sum_kernel(share, out)
    agg = (keep[...] + came[...].astype(jnp.float32)).astype(jnp.bfloat16)
    grad_in[...] = lax.dot_general(
        agg, weight[...], (((1,), (1,)), ((), ())), preferred_element_type=jnp.float32
    ).astype(jnp.bfloat16)


def last_kernel(at, own, other, out):
    k = at[2]
    out[pl.ds(pl.multiple_of(256 * k, 256), 256), :] = own[...].reshape(256, WIDTH).astype(jnp.float32)
    out[pl.ds(pl.multiple_of(256 * (1 - k), 256), 256), :] = other[...].reshape(256, WIDTH).astype(jnp.float32)


def body(grad_out, relu_mask, features, weight, tile_vals, tile_rows, tile_cols, tile_count):
    x, h, k = (lax.axis_index(name) for name in ("x", "h", "k"))
    slope = (grad_out.astype(jnp.float32) * relu_mask.astype(jnp.float32)).astype(jnp.bfloat16)

    slope_h = permute(slope, h_swap)
    own = jnp.stack(around(slope))
    other = permute(own, k_swap)
    own_h = jnp.stack(around(slope_h))
    other_h = permute(own_h, k_swap)
    cols = tile_cols[0, 0]
    places = (cols // 4 - x) % 4 + 4 * ((cols // 2 % 2) ^ h) + 8 * ((cols % 2) ^ k)

    live = jnp.arange(SLOTS, dtype=jnp.int32) < tile_count[0, 0]
    codes = jnp.where(live, tile_rows[0, 0] * 16 + places, 32 * 16)
    at = jnp.stack([lax.axis_index("z"), lax.axis_index("y"), k, tile_count[0, 0]])
    piece = jax.ShapeDtypeStruct((4, 128, WIDTH), jnp.bfloat16)
    first = [
        jax.ShapeDtypeStruct((4, HALF, WIDTH), jnp.bfloat16),
        jax.ShapeDtypeStruct((4, 128 - HALF, WIDTH), jnp.bfloat16),
    ]
    pieces = kernel_call(
        block_kernel,
        first + [piece] * 7,
        [SMEM_SPEC] * 2 + [pl.BlockSpec(memory_space=pl.ANY)] * 5,
        [
            pltpu.VMEM((33, 128, WIDTH), jnp.float32),
            pltpu.VMEM((16, 128, WIDTH), jnp.bfloat16),
            pltpu.VMEM((SLOTS, 128, 128), jnp.bfloat16),
            pltpu.SemaphoreType.DMA((5,)),
        ],
        name="block_terms",
        limit=VMEM_WHOLE,
    )(at, codes, tile_vals[0, 0], own, own_h, other, other_h)

    along = [permute(features, y_from(step)) for step in (1, 2, 3)]
    up, down = pieces[0], pieces[1]
    for step in range(4):
        up, down = permute(up, z_up), permute(down, z_down)
        after = along[step - 1:step] if step else []
        if step == 0:
            up, down = add(pieces[2], up), add(pieces[3], down, HALF)
        elif step < 3:
            up, down = add(pieces[2 + 2 * step], up), add(pieces[3 + 2 * step], down, 0, after)
    parts = (
        pieces[8].astype(jnp.float32) + up.astype(jnp.float32) + down.astype(jnp.float32)
    ).astype(jnp.bfloat16)

    keep, send, across = kernel_call(
        product_kernel,
        (
            jax.ShapeDtypeStruct((256, WIDTH), jnp.float32),
            jax.ShapeDtypeStruct((256, WIDTH), jnp.bfloat16),
            jax.ShapeDtypeStruct((2, 128, WIDTH), jnp.bfloat16),
        ),
        [SMEM_SPEC] + [VMEM_SPEC] * 5,
        [pltpu.VMEM((WIDTH, WIDTH), jnp.float32)],
        name="weight_product",
    )(at, features, *along, parts)
    half = kernel_call(
        half_kernel, jax.ShapeDtypeStruct((32, 8, WIDTH), jnp.bfloat16), [VMEM_SPEC] * 2, name="weight_half"
    )(keep, permute(send, k_swap))
    half = lax.all_to_all(half, ("z", "x"), 0, 0, tiled=True)
    share, keep, send = kernel_call(
        share_kernel,
        (
            jax.ShapeDtypeStruct((8, 8, WIDTH), jnp.bfloat16),
            jax.ShapeDtypeStruct((128, WIDTH), jnp.float32),
            jax.ShapeDtypeStruct((128, WIDTH), jnp.bfloat16),
        ),
        [SMEM_SPEC] + [VMEM_SPEC] * 3,
        name="weight_share",
    )(at, half, parts, permute(across, y_flip(1)))
    send = permute(send, y_flip(2))
    share = lax.all_to_all(share, ("y", "h"), 0, 0, tiled=True)
    half, grad_in = kernel_call(
        total_kernel,
        (jax.ShapeDtypeStruct((32, 8, WIDTH), jnp.bfloat16), jax.ShapeDtypeStruct((128, WIDTH), jnp.bfloat16)),
        [VMEM_SPEC] * 4,
        name="weight_total",
    )(share, keep, send, weight)
    half = lax.all_to_all(half, ("z", "x"), 0, 0, tiled=True)
    grad_weight = kernel_call(
        last_kernel,
        jax.ShapeDtypeStruct((WIDTH, WIDTH), jnp.float32),
        [SMEM_SPEC] + [VMEM_SPEC] * 2,
        name="weight_order",
    )(at, half, permute(half, k_swap))
    return (grad_in, grad_weight)


def solution(mesh):
    fine = Mesh(mesh.devices.reshape(SIZES), AXES)
    nodes = P(AXES, None)
    rows, cols = AXES[:2], AXES[2:]
    return jax.shard_map(
        body,
        mesh=fine,
        in_specs=(
            nodes,
            nodes,
            nodes,
            P(),
            P(rows, cols, None, None, None),
            P(rows, cols, None),
            P(rows, cols, None),
            P(rows, cols),
        ),
        out_specs=(nodes, P()),
        check_vma=False,
    )
```
